32 devices in a mesh: dp: 8 (over z, core), tensor: 4 (over y, x).
Axes of the slice: x: 2, y: 2, z: 4, core: 2. Of those that a mesh axis runs over, the one named last changes fastest.
Arguments:
- hidden: bfloat16 [6144, 2048], P('dp'), may hold values from -6 to 6
- kv_input: bfloat16 [6144, 2048], P('dp'), may hold values from -6 to 6
- attn_norm: float32 [2048], replicated, may hold values from 0.1 to 1.9
- w_query: bfloat16 [2048, 2048], P(None, 'tensor'), may hold values from -0.125 to 0.125
- w_key: bfloat16 [2048, 2048], P(None, 'tensor'), may hold values from -0.125 to 0.125
- w_value: bfloat16 [2048, 2048], P(None, 'tensor'), may hold values from -0.125 to 0.125
- w_out: bfloat16 [2048, 2048], P('tensor'), may hold values from -1 to 1
- kv_norm: float32 [2048], replicated, may hold values from 0.1 to 1.9
- ffn_norm: float32 [2048], replicated, may hold values from 0.1 to 1.9
- w_gate: bfloat16 [2048, 5504], P(None, 'tensor'), may hold values from -0.125 to 0.125
- w_up: bfloat16 [2048, 5504], P(None, 'tensor'), may hold values from -0.125 to 0.125
- w_down: bfloat16 [5504, 2048], P('tensor'), may hold values from -0.078125 to 0.078125
- seq_lengths: int32 [8, 2], P('dp'), may hold values from 0 to 768, as said below
- cotangent: bfloat16 [6144, 2048], P('dp'), may hold values from -6 to 6
Outputs:
- output: bfloat16 [6144, 2048], P('dp')
- grad_input: bfloat16 [6144, 2048], P('dp')
- grad_kv_input: bfloat16 [6144, 2048], P('dp')
- grad_attn_norm: float32 [2048], P('dp')
- grad_query: float32 [2048, 2048], P('dp', 'tensor')
- grad_key: float32 [2048, 2048], P('dp', 'tensor')
- grad_value: float32 [2048, 2048], P('dp', 'tensor')
- grad_out: float32 [2048, 2048], P('tensor', 'dp')
- grad_kv_norm: float32 [2048], P('dp')
- grad_ffn_norm: float32 [2048], P('dp')
- grad_gate: float32 [2048, 5504], P('dp', 'tensor')
- grad_up: float32 [2048, 5504], P('dp', 'tensor')
- grad_down: float32 [5504, 2048], P('tensor', 'dp')
The draws below stay inside these ranges and needn't reach their ends.
Inputs may be any that keep to these rules, and one draw needn't show every extreme that they name: `seq_lengths`: in each row the two lengths sum to 384 or more and to 768 at most, and the first is at least half of that sum, rounded down; in every draw one row holds a single sequence of exactly 768 tokens and a second length 0.
All inputs are finite; a program needn't handle non-finite values.
Results may differ from the reference program's by a relative error of at most 0.015.
Values sent between devices are 32-bit elements; how exact they have to be, the bound alone decides.
A program may use at most 256 MiB of HBM per device.

```python
import jax
import jax.numpy as jnp
from jax import lax

D = 2048
HEADS = 16
HEAD_DIM = 128
FF = 5504
TOK_DEV = 768
TOKENS = 6144
N_DP = 8


def draw_seq_lengths(key, part):
    key = jax.random.fold_in(key, 7)
    key_total, key_full, key_first = jax.random.split(key, 3)
    totals = jax.random.randint(key_total, (N_DP,), TOK_DEV // 2, TOK_DEV + 1)
    full_row = jax.random.randint(key_full, (), 0, N_DP)
    rows = jnp.arange(N_DP, dtype=jnp.int32)
    totals = jnp.where(rows == full_row, TOK_DEV, totals)
    spread = jax.random.randint(key_first, (N_DP,), 0, TOK_DEV + 1)
    firsts = totals // 2 + spread % (totals - totals // 2 + 1)
    firsts = jnp.where(rows == full_row, TOK_DEV, firsts)
    seconds = totals - firsts
    return jnp.stack([firsts, seconds], axis=1).astype(jnp.int32)


def raised(values, stream_key, source, target, shards_of, factor):
    def block_of(dim):
        return (jnp.arange(values.shape[dim]) // (values.shape[dim] // shards_of)).reshape((-1,) + (1,) * (values.ndim - 1 - dim))

    near = jax.random.permutation(stream_key, shards_of)[block_of(target)]
    far = (block_of(target) + shards_of // 2) % shards_of
    return jnp.where((block_of(source) == near) | (block_of(source) == far), factor * values, values)


def levels(stream_key, dims, cuts, smallest, largest):
    level = 1.0
    for axis_at, shards_of in cuts:
        heights = jax.random.uniform(jax.random.fold_in(jax.random.fold_in(stream_key, 6), axis_at), (shards_of,), jnp.float32, smallest / len(cuts), largest / len(cuts))
        level = level * jnp.repeat(jnp.exp(heights), dims[axis_at] // shards_of).reshape((-1,) + (1,) * (len(dims) - 1 - axis_at))
    return level


def scatter_about(stream_key, dims, deviation, most, cuts=(), kind=jnp.bfloat16):
    factor_of = levels(stream_key, dims, cuts, -0.22, 0.18) if cuts else 1.0
    drawn = jax.random.normal(stream_key, dims, jnp.float32) * deviation * factor_of
    return jnp.minimum(jnp.maximum(drawn, -most), most).astype(kind)


def bell_draw_with(rng, extent, scale, reach, pieces, heavy, kind=jnp.bfloat16):
    result = scale * jax.random.normal(rng, extent, jnp.float32)
    if pieces:
        result = result * levels(rng, extent, pieces, -0.22, 0.18)
    return jnp.clip(raised(result, jax.random.fold_in(rng, 3), *heavy), -reach, reach).astype(kind)


def setup_inputs(seed: int = 0) -> dict:
    arg_keys = jax.random.split(jax.random.key(seed), 15)
    hidden = scatter_about(arg_keys[0], (TOKENS, D), 1.0, 6.0, ((0, 8),))
    kv_input = scatter_about(arg_keys[1], (TOKENS, D), 1.0, 6.0, ((0, 8),))
    attn_norm = jnp.clip(1.0 + 0.18 * jax.random.normal(arg_keys[2], (D,), jnp.float32), 0.1, 1.9)
    w_query = scatter_about(arg_keys[3], (D, D), D ** -0.5, 0.125, ((1, 4),))
    w_key = scatter_about(arg_keys[4], (D, D), D ** -0.5, 0.125, ((1, 4),))
    w_value = scatter_about(arg_keys[5], (D, D), D ** -0.5, 0.125, ((1, 4),))
    w_out = scatter_about(arg_keys[6], (D, D), (D // 64) ** -0.5, 1.0, ((0, 4),))
    kv_norm = jnp.clip(1.0 + 0.18 * jax.random.normal(arg_keys[7], (D,), jnp.float32), 0.1, 1.9)
    ffn_norm = jnp.clip(1.0 + 0.18 * jax.random.normal(arg_keys[8], (D,), jnp.float32), 0.1, 1.9)
    w_gate = scatter_about(arg_keys[9], (D, FF), D ** -0.5, 0.125, ((1, 4),))
    w_up = scatter_about(arg_keys[10], (D, FF), D ** -0.5, 0.125, ((1, 4),))
    w_down = scatter_about(arg_keys[11], (FF, D), FF ** -0.5, 0.078125, ((0, 4),))
    seq_lengths = draw_seq_lengths(jax.random.fold_in(arg_keys[14], 71), 0)
    cotangent = bell_draw_with(arg_keys[13], (TOKENS, D), 1.0, 6.0, ((0, 8),), (0, 1, 8, 2.0))
    return dict(hidden=hidden, kv_input=kv_input, attn_norm=attn_norm, w_query=w_query, w_key=w_key, w_value=w_value, w_out=w_out, kv_norm=kv_norm, ffn_norm=ffn_norm, w_gate=w_gate, w_up=w_up, w_down=w_down, seq_lengths=seq_lengths, cotangent=cotangent)


@jax.custom_vjp
def low(v):
    return lax.optimization_barrier(v.astype(jnp.bfloat16)).astype(jnp.float32)

@jax.custom_vjp
def low_back(v):
    return v

def low_keep(v):
    return (low(v), None)

def low_pass(kept, grad):
    return (grad,)

def back_keep(v):
    return (v, None)

def back_low(kept, grad):
    return (low(grad),)
low.defvjp(low_keep, low_pass)
low_back.defvjp(back_keep, back_low)

def rms_unit(values):
    return values * lax.rsqrt(lax.optimization_barrier(jnp.mean(values * values, axis=-1, keepdims=True)) + 1e-06)

def matmul(left, right):
    return jnp.dot(left, right, precision=lax.Precision.HIGHEST)

def attend(block):
    query_b, keys_b, values_b, lens = block
    places = jnp.arange(TOK_DEV, dtype=jnp.int32)
    first = lens[0]
    total = lens[0] + lens[1]
    segment = (places >= first).astype(jnp.int32) + (places >= total).astype(jnp.int32)
    allowed = (segment[:, None] == segment[None, :]) & (places[None, :] <= places[:, None])
    q_heads = query_b.reshape(TOK_DEV, HEADS, HEAD_DIM)
    k_heads = keys_b.reshape(TOK_DEV, HEADS, HEAD_DIM)
    v_heads = values_b.reshape(TOK_DEV, HEADS, HEAD_DIM)
    scores = jnp.einsum('qhd,khd->hqk', q_heads, k_heads, precision=lax.Precision.HIGHEST) * HEAD_DIM ** (-0.5)
    scores = low_back(scores)
    scores = jnp.where(allowed[None], scores, -1e+30)
    probs = low(jax.nn.softmax(scores, axis=-1))
    mixed = jnp.einsum('hqk,khd->qhd', probs, v_heads, precision=lax.Precision.HIGHEST)
    return mixed.reshape(TOK_DEV, D)

def reference(hidden, kv_input, attn_norm, w_query, w_key, w_value, w_out, kv_norm, ffn_norm, w_gate, w_up, w_down, seq_lengths, cotangent):
    places = jnp.arange(TOK_DEV, dtype=jnp.int32)
    totals = seq_lengths[:, 0] + seq_lengths[:, 1]
    live = (places[None, :] < totals[:, None]).astype(jnp.float32).reshape(TOKENS, 1)

    def forward(x_in, kv_in, gain_attn, wq, wk, wv, wo, gain_kv, gain_ffn, wg, wu, wd):
        normed = low(rms_unit(x_in) * gain_attn)
        query = low_back(low(matmul(normed, wq)))
        kv_normed = low(rms_unit(kv_in) * gain_kv)
        keys = low_back(low(matmul(kv_normed, wk)))
        values = low_back(low(matmul(kv_normed, wv)))
        blocks = (query.reshape(N_DP, TOK_DEV, D), keys.reshape(N_DP, TOK_DEV, D), values.reshape(N_DP, TOK_DEV, D), seq_lengths)
        attended = lax.map(jax.checkpoint(attend), blocks).reshape(TOKENS, D)
        attended = low_back(low(attended))
        branch = low_back(matmul(attended, wo))
        resid = x_in + branch
        ffn_in = low(rms_unit(resid) * gain_ffn)
        gate = low_back(matmul(ffn_in, wg))
        up = low_back(matmul(ffn_in, wu))
        activated = low(jax.nn.silu(gate) * up)
        ffn_out = low_back(matmul(activated, wd))
        return (resid + ffn_out) * live
    floats = (hidden.astype(jnp.float32), kv_input.astype(jnp.float32), attn_norm.astype(jnp.float32), w_query.astype(jnp.float32), w_key.astype(jnp.float32), w_value.astype(jnp.float32), w_out.astype(jnp.float32), kv_norm.astype(jnp.float32), ffn_norm.astype(jnp.float32), w_gate.astype(jnp.float32), w_up.astype(jnp.float32), w_down.astype(jnp.float32))
    output, pullback = jax.vjp(forward, *floats)
    grads = pullback(cotangent.astype(jnp.float32))
    return (output.astype(jnp.bfloat16), grads[0].astype(jnp.bfloat16), grads[1].astype(jnp.bfloat16), grads[2], grads[3], grads[4], grads[5], grads[6], grads[7], grads[8], grads[9], grads[10], grads[11])
```

```python
import functools

import jax
import jax.numpy as jnp
from jax import lax
from jax.experimental import pallas as pl
from jax.experimental.pallas import tpu as pltpu
from jax.sharding import PartitionSpec as P

HEAD_DIM = 128
EPS = 1e-06
MESH = pl.DeviceIdType.MESH
ANY = pl.BlockSpec(memory_space=pl.ANY)
F32 = jnp.float32
BF16 = jnp.bfloat16


def norm_scale(values):
    return lax.rsqrt(jnp.mean(values * values, axis=-1, keepdims=True) + EPS)


def left_dot(left, right):
    return lax.dot_general(left, right, (((0,), (0,)), ((), ())), preferred_element_type=F32)


def right_dot(left, right):
    return lax.dot_general(left, right, (((1,), (1,)), ((), ())), preferred_element_type=F32)


def plain_dot(left, right):
    return jnp.dot(left, right, preferred_element_type=F32)


def row_blocks(rows):
    size = 256 if rows % 256 == 0 else rows
    return [(at, size) for at in range(0, rows, size)]


def masked_scores(lens, q, k, start):
    scores = right_dot(q, k) * (HEAD_DIM ** (-0.5))
    first = lens[0, 0]
    total = first + lens[0, 1]
    q_at = start + lax.broadcasted_iota(jnp.int32, (q.shape[0], 1), 0)
    k_at = lax.broadcasted_iota(jnp.int32, (1, k.shape[0]), 1)
    low = jnp.where(q_at >= total, total, jnp.where(q_at >= first, first, 0))
    seen = (k_at <= q_at) & (k_at >= low)
    return jnp.where(seen, scores, -1e30)


def softmax_parts(scores):
    peak = jnp.max(scores, axis=-1, keepdims=True)
    weights = jnp.exp(scores - peak)
    return weights / jnp.sum(weights, axis=-1, keepdims=True)


def attend_kernel(lens, q, k, v, out):
    for at, size in row_blocks(q.shape[0]):
        end = at + size
        probs = softmax_parts(masked_scores(lens, q[at:end, :], k[:end, :], at))
        out[at:end, :] = plain_dot(probs.astype(BF16), v[:end, :]).astype(BF16)


def attend_back_kernel(lens, q, k, v, d_att, d_q, d_k, d_v, k_sum, v_sum):
    scale = HEAD_DIM ** (-0.5)
    k_sum[...] = jnp.zeros_like(k_sum)
    v_sum[...] = jnp.zeros_like(v_sum)
    for at, size in row_blocks(q.shape[0]):
        end = at + size
        probs = softmax_parts(masked_scores(lens, q[at:end, :], k[:end, :], at))
        d_probs = right_dot(d_att[at:end, :], v[:end, :])
        v_sum[:end, :] += left_dot(probs.astype(BF16), d_att[at:end, :])
        inner = jnp.sum(probs * d_probs, axis=-1, keepdims=True)
        d_scores = (probs * (d_probs - inner)).astype(BF16)
        d_q[at:end, :] = (plain_dot(d_scores, k[:end, :]) * scale).astype(BF16)
        k_sum[:end, :] += left_dot(d_scores, q[at:end, :])
    d_k[...] = (k_sum[...] * scale).astype(BF16)
    d_v[...] = v_sum[...].astype(BF16)


def per_head(kernel, n_out, scratch, lens, *arrays):
    rows, width = arrays[0].shape
    spec = pl.BlockSpec((rows, HEAD_DIM), lambda h: (0, h))
    shape = jax.ShapeDtypeStruct((rows, width), BF16)
    return pl.pallas_call(
        kernel,
        grid=(width // HEAD_DIM,),
        in_specs=[pl.BlockSpec(memory_space=pltpu.SMEM)] + [spec] * len(arrays),
        out_specs=[spec] * n_out,
        out_shape=[shape] * n_out,
        scratch_shapes=[pltpu.VMEM((rows, HEAD_DIM), F32)] * scratch,
        compiler_params=pltpu.CompilerParams(vmem_limit_bytes=40 << 20),
        name=kernel.__name__,
    )(lens, *arrays)


class Plane:
    def __init__(self):
        self.me = lax.axis_index("tensor")

    def enter(self):
        barrier = pltpu.get_barrier_semaphore()
        for bit in range(2):
            pl.semaphore_signal(
                barrier, inc=1, device_id={"tensor": self.partner(bit)}, device_id_type=MESH
            )
        pl.semaphore_wait(barrier, 2)

    def mine(self, bit):
        return (self.me // (1 + bit)) % 2

    def partner(self, bit):
        return self.me + (1 - 2 * self.mine(bit)) * (1 + bit)

    def bit(self, chunk, step):
        return (chunk + step) % 2

    def place(self, chunk):
        return 2 * self.mine(self.bit(chunk, 0)) + self.mine(self.bit(chunk, 1))

    def scatter_copy(self, part, recv, send_sem, recv_sem, chunk, step):
        bit = self.bit(chunk, step)
        count = 2 - step
        held = 2 * self.mine(self.bit(chunk, 0)) if step else 0
        src = part.at[chunk, pl.ds(held + (1 - self.mine(bit)) * count, count)]
        return pltpu.make_async_remote_copy(
            src,
            recv[step].at[chunk],
            send_sem.at[chunk, step],
            recv_sem.at[chunk, step],
            device_id={"tensor": self.partner(bit)},
            device_id_type=MESH,
        )

    def gather_copy(self, whole, send_sem, recv_sem, chunk, step):
        bit = self.bit(chunk, step)
        count = 2 - step
        held = self.place(chunk) if step else 2 * self.mine(bit)
        ref = whole.at[chunk, pl.ds(held, count)]
        return pltpu.make_async_remote_copy(
            ref,
            ref,
            send_sem.at[chunk, step],
            recv_sem.at[chunk, step],
            device_id={"tensor": self.partner(bit)},
            device_id_type=MESH,
        )

    def halve(self, part, recv, send_sem, recv_sem, chunk):
        self.scatter_copy(part, recv, send_sem, recv_sem, chunk, 0).wait_recv()
        held = 2 * self.mine(self.bit(chunk, 0))
        for piece in range(2):
            part[chunk, held + piece] += recv[0][chunk, piece]
        self.scatter_copy(part, recv, send_sem, recv_sem, chunk, 1).start()

    def total(self, part, recv, send_sem, recv_sem, chunk):
        self.scatter_copy(part, recv, send_sem, recv_sem, chunk, 1).wait_recv()
        return part[chunk, self.place(chunk)] + recv[1][chunk, 0]


def own_pieces(array, chunks):
    rows, width = array.shape
    me = lax.axis_index("tensor")
    low, high = me % 2, me // 2
    pieces = array.reshape(chunks // 2, 2, 4, rows // chunks // 4, width)
    even = lax.dynamic_index_in_dim(pieces[:, 0], 2 * low + high, 1, keepdims=False)
    odd = lax.dynamic_index_in_dim(pieces[:, 1], 2 * high + low, 1, keepdims=False)
    return jnp.stack([even, odd], axis=1).reshape(chunks, -1, width).astype(F32)


def tiles(width, size):
    return [(at, min(at + size, width)) for at in range(0, width, size)]


def column_tiles(width):
    return tiles(width, 512)


def ffn_kernel(
    chunks,
    att_h, x_own_h, d_low_h, gain_h, w_out_h, w_gate_h, w_up_h, w_down_h,
    ffn_in_h, act_h, dg_h, du_h, d_res_h, resid_h, gain_grad_h,
    att, x_own, d_low, gain, w_out, w_gate, w_up, w_down,
    ffn_in, act, dg, du, gain_grad, scale,
    part, whole, recv0, recv1, send_sem, recv_sem, load_sem, store_sem, piece_sem,
):
    plane = Plane()
    recv = (recv0, recv1)
    rows = chunks * part.shape[1] * part.shape[2]
    size = rows // chunks
    width = part.shape[3]
    hidden = act.shape[1]
    loads = [
        pltpu.make_async_copy(src, dst, load_sem.at[i])
        for i, (src, dst) in enumerate(
            [
                (att_h, att), (w_out_h, w_out), (x_own_h, x_own), (gain_h, gain),
                (w_gate_h, w_gate), (w_up_h, w_up), (w_down_h, w_down), (d_low_h, d_low),
            ]
        )
    ]
    for load in loads:
        load.start()
    gain_grad[...] = jnp.zeros_like(gain_grad)
    plane.enter()
    loads[0].wait()
    loads[1].wait()

    def rows_of(c):
        return pl.ds(pl.multiple_of(c * size, size), size)

    def scatter(phase, c, step):
        return plane.scatter_copy(part, recv, send_sem.at[phase], recv_sem.at[phase], c, step)

    def gather(phase, ref, c, step):
        return plane.gather_copy(ref, send_sem.at[phase], recv_sem.at[phase], c, step)

    @pl.loop(0, chunks)
    def _(c):
        left = att[rows_of(c), :]
        for a, b in column_tiles(width):
            part[c, :, :, a:b] = plain_dot(left, w_out[:, a:b]).reshape(4, size // 4, b - a)
        scatter(0, c, 0).start()

    loads[2].wait()
    loads[3].wait()

    @pl.loop(0, chunks)
    def _(c):
        plane.halve(part, recv, send_sem.at[0], recv_sem.at[0], c)

    @pl.loop(0, chunks)
    def _(c):
        resid = x_own[c] + plane.total(part, recv, send_sem.at[0], recv_sem.at[0], c)
        x_own[c] = resid
        scale[c] = norm_scale(resid)
        whole[c, plane.place(c)] = resid * scale[c]
        gather(1, whole, c, 1).start()

    @pl.loop(0, chunks)
    def _(c):
        gather(1, whole, c, 1).wait_recv()
        gather(1, whole, c, 0).start()

    for load in loads[4:]:
        load.wait()
    store_resid = pltpu.make_async_copy(x_own, resid_h, store_sem.at[0])
    store_resid.start()

    @pl.loop(0, chunks)
    def _(c):
        gather(1, whole, c, 0).wait_recv()
        for piece in range(4):
            at = pl.ds(pl.multiple_of(c * size + piece * (size // 4), size // 4), size // 4)
            ffn_in[at, :] = (whole[c, piece] * gain[...]).astype(BF16)
        left = ffn_in[rows_of(c), :]
        for a, b in column_tiles(hidden):
            gate = plain_dot(left, w_gate[:, a:b])
            up = plain_dot(left, w_up[:, a:b])
            d_act = right_dot(d_low[rows_of(c), :], w_down[a:b, :])
            sigma = jax.nn.sigmoid(gate)
            act[rows_of(c), a:b] = (gate * sigma * up).astype(BF16)
            dg[rows_of(c), a:b] = (d_act * up * sigma * (1.0 + gate * (1.0 - sigma))).astype(BF16)
            du[rows_of(c), a:b] = (d_act * gate * sigma).astype(BF16)
        for step in range(2):
            scatter(0, c, step).wait_send()
        for a, b in column_tiles(width):
            sums = right_dot(dg[rows_of(c), :], w_gate[a:b, :]) + right_dot(du[rows_of(c), :], w_up[a:b, :])
            part[c, :, :, a:b] = sums.reshape(4, size // 4, b - a)
        scatter(2, c, 0).start()

    stores = [
        pltpu.make_async_copy(src, dst, store_sem.at[1 + i])
        for i, (src, dst) in enumerate([(ffn_in, ffn_in_h), (act, act_h), (dg, dg_h), (du, du_h)])
    ]
    for store in stores:
        store.start()

    @pl.loop(0, chunks)
    def _(c):
        plane.halve(part, recv, send_sem.at[2], recv_sem.at[2], c)

    @pl.loop(0, chunks)
    def _(c):
        d_in = plane.total(part, recv, send_sem.at[2], recv_sem.at[2], c)
        unit = whole[c, plane.place(c)]
        gain_grad[...] += jnp.sum(d_in * unit, axis=0, keepdims=True)
        d_unit = d_in * gain[...]
        mean = jnp.mean(d_unit * unit, axis=-1, keepdims=True)
        part[c, plane.place(c)] = scale[c] * (d_unit - unit * mean)
        piece = pltpu.make_async_copy(
            part.at[c, plane.place(c)], d_res_h.at[c, plane.place(c)], piece_sem
        )
        piece.start()
        piece.wait()
        gather(3, d_res_h, c, 1).start()

    store_gain = pltpu.make_async_copy(gain_grad, gain_grad_h, store_sem.at[5])
    store_gain.start()

    @pl.loop(0, chunks)
    def _(c):
        gather(3, d_res_h, c, 1).wait_recv()
        gather(3, d_res_h, c, 0).start()

    @pl.loop(0, chunks)
    def _(c):
        gather(3, d_res_h, c, 0).wait_recv()
        for step in range(2):
            gather(1, whole, c, step).wait_send()
            scatter(2, c, step).wait_send()
            gather(3, d_res_h, c, step).wait_send()

    store_resid.wait()
    store_gain.wait()
    for store in stores:
        store.wait()


def ffn_call(chunks, att, x_own, d_low, gain, w_out, w_gate, w_up, w_down):
    rows, inner = att.shape
    width = w_out.shape[1]
    hidden = w_gate.shape[1]
    piece = rows // chunks // 4
    out = jax.ShapeDtypeStruct
    pieces = (chunks, 4, piece, width)
    return pl.pallas_call(
        functools.partial(ffn_kernel, chunks),
        in_specs=[ANY] * 8,
        out_specs=[ANY] * 7,
        out_shape=[
            out((rows, width), BF16),
            out((rows, hidden), BF16),
            out((rows, hidden), BF16),
            out((rows, hidden), BF16),
            out(pieces, F32),
            out((chunks, piece, width), F32),
            out((1, width), F32),
        ],
        scratch_shapes=[
            pltpu.VMEM((rows, inner), BF16),
            pltpu.VMEM((chunks, piece, width), F32),
            pltpu.VMEM((rows, width), BF16),
            pltpu.VMEM((1, width), F32),
            pltpu.VMEM((inner, width), BF16),
            pltpu.VMEM((width, hidden), BF16),
            pltpu.VMEM((width, hidden), BF16),
            pltpu.VMEM((hidden, width), BF16),
            pltpu.VMEM((rows, width), BF16),
            pltpu.VMEM((rows, hidden), BF16),
            pltpu.VMEM((rows, hidden), BF16),
            pltpu.VMEM((rows, hidden), BF16),
            pltpu.VMEM((1, width), F32),
            pltpu.VMEM((chunks, piece, 1), F32),
            pltpu.VMEM(pieces, F32),
            pltpu.VMEM(pieces, F32),
            pltpu.VMEM((chunks, 2, piece, width), F32),
            pltpu.VMEM((chunks, 1, piece, width), F32),
            pltpu.SemaphoreType.DMA((4, chunks, 2)),
            pltpu.SemaphoreType.DMA((4, chunks, 2)),
            pltpu.SemaphoreType.DMA((8,)),
            pltpu.SemaphoreType.DMA((6,)),
            pltpu.SemaphoreType.DMA,
        ],
        compiler_params=pltpu.CompilerParams(
            collective_id=0, has_side_effects=True, vmem_limit_bytes=63 << 20
        ),
        name="ffn",
    )(att, x_own, d_low, gain, w_out, w_gate, w_up, w_down)


def last_kernel(
    chunks,
    act_h, w_down_h, resid_h, dq_h, dk_h, dv_h, w_q_h, w_k_h, w_v_h, x_own_h, kv_own_h, gain_x_h, gain_kv_h,
    out_h, d_x_h, d_kv_h, gain_grad_h,
    act, w_down, resid, dq, dk, dv, w_q, w_k, w_v, x_own, kv_own, gain_x, gain_kv,
    gain_grad, part_a, part_b, part_c, recv_a0, recv_a1, recv_b0, recv_b1, recv_c0, recv_c1,
    send_sem, recv_sem, load_sem, store_sem, piece_sem,
):
    plane = Plane()
    size = part_a.shape[1] * part_a.shape[2]
    width = part_a.shape[3]
    loads = [
        pltpu.make_async_copy(src, dst, load_sem.at[i])
        for i, (src, dst) in enumerate(
            [
                (act_h, act), (w_down_h, w_down), (dq_h, dq), (w_q_h, w_q), (dk_h, dk), (dv_h, dv), (w_k_h, w_k),
                (w_v_h, w_v), (resid_h, resid), (x_own_h, x_own), (kv_own_h, kv_own), (gain_x_h, gain_x),
                (gain_kv_h, gain_kv),
            ]
        )
    ]
    for load in loads:
        load.start()
    gain_grad[...] = jnp.zeros_like(gain_grad)
    plane.enter()

    def rows_of(c):
        return pl.ds(pl.multiple_of(c * size, size), size)

    sets = ((part_a, (recv_a0, recv_a1), out_h), (part_b, (recv_b0, recv_b1), d_x_h), (part_c, (recv_c0, recv_c1), d_kv_h))

    def scatter(which, c, step):
        part, recv, _ = sets[which]
        return plane.scatter_copy(part, recv, send_sem.at[which], recv_sem.at[which], c, step)

    def gather(which, c, step):
        return plane.gather_copy(sets[which][2], send_sem.at[3 + which], recv_sem.at[3 + which], c, step)

    for load in loads[:2]:
        load.wait()

    @pl.loop(0, chunks)
    def _(c):
        for a, b in column_tiles(width):
            sums = plain_dot(act[rows_of(c), :], w_down[:, a:b])
            part_a[c, :, :, a:b] = sums.reshape(4, size // 4, b - a)
        scatter(0, c, 0).start()

    for load in loads[2:4]:
        load.wait()

    @pl.loop(0, chunks)
    def _(c):
        for a, b in column_tiles(width):
            sums = right_dot(dq[rows_of(c), :], w_q[a:b, :])
            part_b[c, :, :, a:b] = sums.reshape(4, size // 4, b - a)
        scatter(1, c, 0).start()

    for load in loads[4:8]:
        load.wait()

    @pl.loop(0, chunks)
    def _(c):
        for a, b in column_tiles(width):
            sums = right_dot(dk[rows_of(c), :], w_k[a:b, :]) + right_dot(dv[rows_of(c), :], w_v[a:b, :])
            part_c[c, :, :, a:b] = sums.reshape(4, size // 4, b - a)
        scatter(2, c, 0).start()

    for load in loads[8:]:
        load.wait()

    def finish(which, c):
        part, recv, whole = sets[which]
        got = plane.total(part, recv, send_sem.at[which], recv_sem.at[which], c)
        if which == 0:
            part[c, plane.place(c)] = resid[c] + got
        else:
            own, gain = ((x_own, gain_x), (kv_own, gain_kv))[which - 1]
            scale = norm_scale(own[c])
            unit = own[c] * scale
            gain_grad[which - 1] += jnp.sum(got * unit, axis=0, keepdims=True)
            d_unit = got * gain[...]
            mean = jnp.mean(d_unit * unit, axis=-1, keepdims=True)
            part[c, plane.place(c)] = scale * (d_unit - unit * mean)
        piece = pltpu.make_async_copy(part.at[c, plane.place(c)], whole.at[c, plane.place(c)], piece_sem)
        piece.start()
        piece.wait()
        gather(which, c, 1).start()

    for which in range(3):
        part, recv, _ = sets[which]

        @pl.loop(0, chunks)
        def _(c):
            plane.halve(part, recv, send_sem.at[which], recv_sem.at[which], c)

    for which in range(3):

        @pl.loop(0, chunks)
        def _(c):
            finish(which, c)

    store_gain = pltpu.make_async_copy(gain_grad, gain_grad_h, store_sem)
    store_gain.start()

    for which in range(3):

        @pl.loop(0, chunks)
        def _(c):
            gather(which, c, 1).wait_recv()
            gather(which, c, 0).start()

    for which in range(3):

        @pl.loop(0, chunks)
        def _(c):
            gather(which, c, 0).wait_recv()
            for step in range(2):
                scatter(which, c, step).wait_send()
                gather(which, c, step).wait_send()

    store_gain.wait()


def last_call(chunks, act, w_down, resid, dq, dk, dv, w_q, w_k, w_v, x_own, kv_own, gain_x, gain_kv):
    rows, hidden = act.shape
    inner = dq.shape[1]
    width = w_down.shape[1]
    piece = rows // chunks // 4
    out = jax.ShapeDtypeStruct
    pieces = (chunks, 4, piece, width)
    own = pltpu.VMEM((chunks, piece, width), F32)
    return pl.pallas_call(
        functools.partial(last_kernel, chunks),
        in_specs=[ANY] * 13,
        out_specs=[ANY] * 4,
        out_shape=[out(pieces, F32), out(pieces, F32), out(pieces, F32), out((2, 1, width), F32)],
        scratch_shapes=[
            pltpu.VMEM((rows, hidden), BF16),
            pltpu.VMEM((hidden, width), BF16),
            own,
            pltpu.VMEM((rows, inner), BF16),
            pltpu.VMEM((rows, inner), BF16),
            pltpu.VMEM((rows, inner), BF16),
            pltpu.VMEM((width, inner), BF16),
            pltpu.VMEM((width, inner), BF16),
            pltpu.VMEM((width, inner), BF16),
            own,
            own,
            pltpu.VMEM((1, width), F32),
            pltpu.VMEM((1, width), F32),
            pltpu.VMEM((2, 1, width), F32),
            pltpu.VMEM(pieces, F32),
            pltpu.VMEM(pieces, F32),
            pltpu.VMEM(pieces, F32),
        ]
        + [pltpu.VMEM((chunks, 2, piece, width), F32), pltpu.VMEM((chunks, 1, piece, width), F32)] * 3
        + [
            pltpu.SemaphoreType.DMA((6, chunks, 2)),
            pltpu.SemaphoreType.DMA((6, chunks, 2)),
            pltpu.SemaphoreType.DMA((13,)),
            pltpu.SemaphoreType.DMA,
            pltpu.SemaphoreType.DMA,
        ],
        compiler_params=pltpu.CompilerParams(
            collective_id=1, has_side_effects=True, vmem_limit_bytes=63 << 20
        ),
        cost_estimate=pl.CostEstimate(flops=3 * 10**11, bytes_accessed=10**8, transcendentals=0),
        name="last",
    )(act, w_down, resid, dq, dk, dv, w_q, w_k, w_v, x_own, kv_own, gain_x, gain_kv)


CHUNKS = 4


def body(
    hidden, kv_input, attn_norm, w_query, w_key, w_value, w_out, kv_norm, ffn_norm, w_gate, w_up, w_down, seq_lengths, cotangent
):
    rows, width = hidden.shape
    total = seq_lengths[0, 0] + seq_lengths[0, 1]
    live = (jnp.arange(rows, dtype=jnp.int32) < total).astype(F32)[:, None]

    x_full = hidden.astype(F32)
    normed = (x_full * norm_scale(x_full) * attn_norm).astype(BF16)
    query = plain_dot(normed, w_query).astype(BF16)
    kv_full = kv_input.astype(F32)
    scale_kv = norm_scale(kv_full)
    kv_normed = (kv_full * scale_kv * kv_norm).astype(BF16)
    keys = plain_dot(kv_normed, w_key).astype(BF16)
    values = plain_dot(kv_normed, w_value).astype(BF16)
    (attended,) = per_head(attend_kernel, 1, 0, seq_lengths, query, keys, values)

    d_out = cotangent.astype(F32) * live
    d_out_low = d_out.astype(BF16)
    x_own = own_pieces(hidden, CHUNKS)
    kv_own = own_pieces(kv_input, CHUNKS)
    ffn_in, activated, d_gate, d_up, d_res, resid_own, grad_ffn_norm = ffn_call(
        CHUNKS, attended, x_own, d_out_low, ffn_norm[None], w_out, w_gate, w_up, w_down
    )

    g_gate, g_up, g_down = left_dot(ffn_in, d_gate), left_dot(ffn_in, d_up), left_dot(activated, d_out_low)
    g_gate, g_up, g_down, d_res = lax.optimization_barrier((g_gate, g_up, g_down, d_res))
    grad_gate = lax.psum_scatter(g_gate, "dp", scatter_dimension=0, tiled=True)
    grad_up = lax.psum_scatter(g_up, "dp", scatter_dimension=0, tiled=True)
    grad_down = lax.psum_scatter(g_down, "dp", scatter_dimension=1, tiled=True)

    d_resid = d_out + d_res.reshape(rows, width)
    d_branch = d_resid.astype(BF16)
    grad_out = lax.psum_scatter(left_dot(attended, d_branch), "dp", scatter_dimension=1, tiled=True)
    d_att = right_dot(d_branch, w_out).astype(BF16)
    d_query, d_keys, d_values = per_head(attend_back_kernel, 3, 2, seq_lengths, query, keys, values, d_att)
    g_query, g_key, g_value = left_dot(normed, d_query), left_dot(kv_normed, d_keys), left_dot(kv_normed, d_values)
    g_query, g_key, g_value, d_query = lax.optimization_barrier((g_query, g_key, g_value, d_query))
    grad_query = lax.psum_scatter(g_query, "dp", scatter_dimension=0, tiled=True)
    grad_key = lax.psum_scatter(g_key, "dp", scatter_dimension=0, tiled=True)
    grad_value = lax.psum_scatter(g_value, "dp", scatter_dimension=0, tiled=True)

    summed, d_x, d_kv, grad_norms = last_call(
        CHUNKS, activated, w_down, resid_own, d_query, d_keys, d_values, w_query, w_key, w_value, x_own, kv_own,
        attn_norm[None], kv_norm[None],
    )
    output = (summed.reshape(rows, width) * live).astype(BF16)
    grad_input = (d_resid + d_x.reshape(rows, width)).astype(BF16)
    grad_kv_input = d_kv.reshape(rows, width).astype(BF16)

    gains = jnp.stack([grad_norms[0, 0], grad_norms[1, 0], grad_ffn_norm[0]])
    gains = lax.psum_scatter(lax.psum(gains, "tensor"), "dp", scatter_dimension=1, tiled=True)
    return (
        output, grad_input, grad_kv_input, gains[0], grad_query, grad_key, grad_value, grad_out, gains[1], gains[2],
        grad_gate, grad_up, grad_down,
    )


def norm_back(d_normed, unit, scale_row, gain):
    gain_grad = jnp.sum(d_normed * unit, axis=0)
    d_unit = d_normed * gain
    d_in = scale_row * (d_unit - unit * jnp.mean(d_unit * unit, axis=-1, keepdims=True))
    return (gain_grad, d_in)


def plain_body(
    hidden,
    kv_input,
    attn_norm,
    w_query,
    w_key,
    w_value,
    w_out,
    kv_norm,
    ffn_norm,
    w_gate,
    w_up,
    w_down,
    seq_lengths,
    cotangent,
):
    rows = hidden.shape[0]
    width = w_query.shape[1]
    heads = width // HEAD_DIM
    scale = HEAD_DIM ** (-0.5)
    first = seq_lengths[0, 0]
    total = first + seq_lengths[0, 1]
    places = jnp.arange(rows, dtype=jnp.int32)
    segment = (places >= first).astype(jnp.int32) + (places >= total).astype(jnp.int32)
    allowed = (segment[:, None] == segment[None, :]) & (places[None, :] <= places[:, None])
    live = (places < total).astype(F32)[:, None]
    x_full = hidden.astype(F32)
    scale_attn = norm_scale(x_full)
    unit_attn = x_full * scale_attn
    normed = (unit_attn * attn_norm).astype(BF16)
    query = jnp.dot(normed, w_query, preferred_element_type=F32).astype(BF16)
    kv_full = kv_input.astype(F32)
    scale_kv = norm_scale(kv_full)
    unit_kv = kv_full * scale_kv
    kv_normed = (unit_kv * kv_norm).astype(BF16)
    keys = jnp.dot(kv_normed, w_key, preferred_element_type=F32).astype(BF16)
    values = jnp.dot(kv_normed, w_value, preferred_element_type=F32).astype(BF16)
    q_heads = query.reshape(rows, heads, HEAD_DIM)
    k_heads = keys.reshape(rows, heads, HEAD_DIM)
    v_heads = values.reshape(rows, heads, HEAD_DIM)

    def scores_of():
        raw = (
            jnp.einsum("qhd,khd->hqk", q_heads, k_heads, preferred_element_type=F32) * scale
        )
        return jnp.where(allowed[None], raw, -1e30)

    scores = scores_of()
    peak = jnp.max(scores, axis=-1, keepdims=True)
    weights = jnp.exp(scores - peak)
    row_total = jnp.sum(weights, axis=-1, keepdims=True)
    log_total = peak + jnp.log(row_total)
    probs_low = (weights / row_total).astype(BF16)
    attended = jnp.einsum("hqk,khd->qhd", probs_low, v_heads, preferred_element_type=F32)
    attended = attended.astype(BF16).reshape(rows, width)
    branch = lax.psum(jnp.dot(attended, w_out, preferred_element_type=F32), "tensor")
    resid = x_full + branch
    scale_ffn = norm_scale(resid)
    unit_ffn = resid * scale_ffn
    ffn_in = (unit_ffn * ffn_norm).astype(BF16)
    gate_pre, up_pre = (
        jnp.dot(ffn_in, w_gate, preferred_element_type=F32),
        jnp.dot(ffn_in, w_up, preferred_element_type=F32),
    )
    activated = (jax.nn.silu(gate_pre) * up_pre).astype(BF16)
    ffn_out = lax.psum(jnp.dot(activated, w_down, preferred_element_type=F32), "tensor")
    output = ((resid + ffn_out) * live).astype(BF16)
    d_out = cotangent.astype(F32) * live
    d_out_low = d_out.astype(BF16)
    grad_down = left_dot(activated, d_out_low)
    d_act = right_dot(d_out_low, w_down)
    gate_use, up_use = (gate_pre, up_pre)
    sigma = jax.nn.sigmoid(gate_use)
    d_gate = (d_act * up_use * sigma * (1.0 + gate_use * (1.0 - sigma))).astype(BF16)
    d_up = (d_act * gate_use * sigma).astype(BF16)
    grad_gate = left_dot(ffn_in, d_gate)
    grad_up = left_dot(ffn_in, d_up)
    d_ffn_in = lax.psum(right_dot(d_gate, w_gate) + right_dot(d_up, w_up), "tensor")
    grad_ffn_norm, d_res_norm = norm_back(d_ffn_in, unit_ffn, scale_ffn, ffn_norm)
    d_resid = d_out + d_res_norm
    d_branch = d_resid.astype(BF16)
    grad_out = left_dot(attended, d_branch)
    d_att = right_dot(d_branch, w_out).astype(BF16).reshape(rows, heads, HEAD_DIM)
    probs = jnp.exp(scores_of() - log_total)
    probs_back = probs.astype(BF16)
    d_probs = jnp.einsum("qhd,khd->hqk", d_att, v_heads, preferred_element_type=F32)
    d_values = jnp.einsum("hqk,qhd->khd", probs_back, d_att, preferred_element_type=F32)
    d_values = d_values.astype(BF16).reshape(rows, width)
    inner = jnp.sum(probs * d_probs, axis=-1, keepdims=True)
    d_scores = (probs * (d_probs - inner)).astype(BF16)
    d_query = (
        jnp.einsum("hqk,khd->qhd", d_scores, k_heads, preferred_element_type=F32) * scale
    )
    d_query = d_query.astype(BF16).reshape(rows, width)
    d_keys = (
        jnp.einsum("hqk,qhd->khd", d_scores, q_heads, preferred_element_type=F32) * scale
    )
    d_keys = d_keys.astype(BF16).reshape(rows, width)
    grad_query = left_dot(normed, d_query)
    grad_key = left_dot(kv_normed, d_keys)
    grad_value = left_dot(kv_normed, d_values)
    d_normed, d_kv_normed = lax.psum(
        (right_dot(d_query, w_query), right_dot(d_keys, w_key) + right_dot(d_values, w_value)),
        "tensor",
    )
    grad_attn_norm, d_x = norm_back(d_normed, unit_attn, scale_attn, attn_norm)
    grad_kv_norm, d_kv = norm_back(d_kv_normed, unit_kv, scale_kv, kv_norm)
    grad_input = (d_resid + d_x).astype(BF16)
    grad_kv_input = d_kv.astype(BF16)
    parts = (
        lax.psum_scatter(grad_attn_norm, "dp", scatter_dimension=0, tiled=True),
        lax.psum_scatter(grad_query, "dp", scatter_dimension=0, tiled=True),
        lax.psum_scatter(grad_key, "dp", scatter_dimension=0, tiled=True),
        lax.psum_scatter(grad_value, "dp", scatter_dimension=0, tiled=True),
        lax.psum_scatter(grad_out, "dp", scatter_dimension=1, tiled=True),
        lax.psum_scatter(grad_kv_norm, "dp", scatter_dimension=0, tiled=True),
        lax.psum_scatter(grad_ffn_norm, "dp", scatter_dimension=0, tiled=True),
        lax.psum_scatter(grad_gate, "dp", scatter_dimension=0, tiled=True),
        lax.psum_scatter(grad_up, "dp", scatter_dimension=0, tiled=True),
        lax.psum_scatter(grad_down, "dp", scatter_dimension=1, tiled=True),
    )
    return (
        output,
        grad_input,
        grad_kv_input,
        parts[0],
        parts[1],
        parts[2],
        parts[3],
        parts[4],
        parts[5],
        parts[6],
        parts[7],
        parts[8],
        parts[9],
    )


def solution(mesh):
    in_specs = (
        P("dp", None), P("dp", None), P(), P(None, "tensor"), P(None, "tensor"), P(None, "tensor"), P("tensor", None),
        P(), P(), P(None, "tensor"), P(None, "tensor"), P("tensor", None), P("dp", None), P("dp", None),
    )
    out_specs = (
        P("dp", None), P("dp", None), P("dp", None), P("dp"), P("dp", "tensor"), P("dp", "tensor"), P("dp", "tensor"),
        P("tensor", "dp"), P("dp"), P("dp"), P("dp", "tensor"), P("dp", "tensor"), P("tensor", "dp"),
    )
    program = body if mesh.shape["tensor"] == 4 else plain_body
    return jax.shard_map(program, mesh=mesh, in_specs=in_specs, out_specs=out_specs, check_vma=False)
```
